32 devices in a mesh: row: 16 (over z, y, core), col: 2 (over x).
Axes of the slice: x: 2, y: 2, z: 4, core: 2. Of those that a mesh axis runs over, the one named last changes fastest.
Arguments:
- features: bfloat16 [12288, 512], P(('row', 'col')), may hold values from -6 to 6
- weight: bfloat16 [512, 512], replicated, may hold values from -0.25 to 0.25
- tile_values: bfloat16 [16, 2, 8, 128, 128], P('row', 'col'), may hold values from -0.3125 to 0.3125
- tile_rows: int32 [16, 2, 8], P('row', 'col'), may hold values from 0 to 5, as said below
- tile_cols: int32 [16, 2, 8], P('row', 'col'), may hold values from 0 to 47, as said below
- tile_count: int32 [16, 2], P('row', 'col'), may hold values from 1 to 8, as said below
- cotangent: bfloat16 [12288, 512], P(('row', 'col')), may hold values from -6 to 6
Outputs:
- activated: bfloat16 [12288, 512], P(('row', 'col'))
- grad_features: bfloat16 [12288, 512], P(('row', 'col'))
- grad_weight: float32 [512, 512], replicated
The draws below stay inside these ranges and needn't reach their ends.
Inputs may be any that keep to these rules, and one draw needn't show every extreme that they name: `tile_rows`: within one block the live and dead slots name distinct tiles. `tile_cols`: within one block the live and dead slots name distinct tiles. `tile_count`: some block has all 8 slots live.
All inputs are finite; a program needn't handle non-finite values.
Results may differ from the reference program's by a relative error of at most 0.012.
Values may be sent and summed in bfloat16 or wider, within the bound.
A program may use at most 128 MiB of HBM per device.

```python
import jax
import jax.numpy as jnp
from jax import lax

F = 512
TILE = 128
ROWS_DEV = 384
NODES = 12288
ROW_TILES = 6
COL_TILES = 48
SLOTS = 8
N_ROW = 16
N_COL = 2


def tile_cells(key):
    all_keys = jax.random.split(key, N_ROW * N_COL)
    chosen_cells = jax.vmap(lambda one_key: jax.random.permutation(one_key, ROW_TILES * COL_TILES))(all_keys)
    return chosen_cells[:, :SLOTS].reshape(N_ROW, N_COL, SLOTS).astype(jnp.int32)


def draw_tile_rows(key, part):
    chosen_cells = tile_cells(key)
    return (chosen_cells // COL_TILES).astype(jnp.int32)


def draw_tile_cols(key, part):
    chosen_cells = tile_cells(key)
    return (chosen_cells % COL_TILES).astype(jnp.int32)


def draw_tile_count(key, part):
    key = jax.random.fold_in(key, 3)
    key_one, key_two, key_three = jax.random.split(key, 3)
    factor_one = jax.random.randint(key_one, (N_ROW * N_COL,), 0, SLOTS + 1)
    factor_two = jax.random.randint(key_two, (N_ROW * N_COL,), 0, SLOTS + 1)
    counts = jnp.maximum(SLOTS // 8, factor_one * factor_two // SLOTS)
    chosen = jax.random.randint(key_three, (), 0, N_ROW * N_COL)
    counts = jnp.where(jnp.arange(N_ROW * N_COL) == chosen, SLOTS, counts)
    return counts.reshape(N_ROW, N_COL).astype(jnp.int32)


def levels(stream_key, shape, cuts, smallest, largest):
    gain, own = 1.0, jax.random.fold_in(stream_key, 6)
    for dim, shards_of in cuts:
        steps = jnp.exp(jax.random.uniform(jax.random.fold_in(own, dim), (shards_of,), jnp.float32, smallest / len(cuts), largest / len(cuts)))
        gain = gain * jnp.repeat(steps, shape[dim] // shards_of).reshape([-1 if axis == dim else 1 for axis in range(len(shape))])
    return gain


def noise(rng, extent, spread, bound, shards=(), held_as=jnp.bfloat16):
    result = jax.random.normal(rng, extent, jnp.float32) * spread
    if len(shards) > 0:
        result = levels(rng, extent, shards, -0.22, 0.18) * result
    return jnp.clip(result, min=-bound, max=bound).astype(held_as)


def setup_inputs(seed: int = 0) -> dict:
    arg_keys = jax.random.split(jax.random.key(seed), 8)
    features = noise(arg_keys[0], (NODES, F), 1.0, 6.0, ((0, 32),))
    weight = noise(arg_keys[1], (F, F), F ** -0.5, 0.25)
    tile_values = noise(arg_keys[2], (N_ROW, N_COL, SLOTS, TILE, TILE), (TILE * SLOTS * N_COL // ROW_TILES) ** -0.5, 0.3125, ((0, 16), (1, 2)))
    tile_rows = draw_tile_rows(jax.random.fold_in(arg_keys[7], 71), 0)
    tile_cols = draw_tile_cols(jax.random.fold_in(arg_keys[7], 71), 0)
    tile_count = draw_tile_count(jax.random.fold_in(arg_keys[7], 71), 0)
    cotangent = noise(arg_keys[6], (NODES, F), 1.0, 6.0, ((0, 32),))
    return {"features": features, "weight": weight, "tile_values": tile_values, "tile_rows": tile_rows, "tile_cols": tile_cols, "tile_count": tile_count, "cotangent": cotangent}


def gelu_tanh(field):
    return jax.nn.gelu(field, approximate=True)

def reference(features, weight, tile_values, tile_rows, tile_cols, tile_count, cotangent):
    hidden = jnp.dot(features, weight, preferred_element_type=jnp.float32).astype(jnp.bfloat16)
    col_blocks = hidden.reshape(N_ROW, N_COL, ROWS_DEV, F).transpose(1, 0, 2, 3).reshape(N_COL, COL_TILES, TILE, F)

    def forward_step(device_index, totals):
        grid_row = device_index // N_COL
        grid_col = device_index % N_COL
        block_values = tile_values[grid_row, grid_col].astype(jnp.float32)
        sources = col_blocks[grid_col][tile_cols[grid_row, grid_col]].astype(jnp.float32)
        products = jnp.einsum('kij,kjf->kif', block_values, sources, precision=lax.Precision.HIGHEST)
        active = jnp.arange(SLOTS) < tile_count[grid_row, grid_col]
        onehot = ((tile_rows[grid_row, grid_col][:, None] == jnp.arange(ROW_TILES)[None, :]) & active[:, None]).astype(jnp.float32)
        partial_value = jnp.einsum('kg,kif->gif', onehot, products, precision=lax.Precision.HIGHEST)
        return totals.at[grid_row].add(partial_value)
    totals = lax.fori_loop(0, N_ROW * N_COL, forward_step, jnp.zeros((N_ROW, ROW_TILES, TILE, F), jnp.float32))
    summed = totals.reshape(NODES, F)
    activated = gelu_tanh(summed).astype(jnp.bfloat16)
    _, pullback = jax.vjp(gelu_tanh, summed)
    slope = pullback(cotangent.astype(jnp.float32))[0].astype(jnp.bfloat16)
    row_blocks = slope.reshape(N_ROW, ROW_TILES, TILE, F)

    def backward_step(device_index, totals_back):
        grid_row = device_index // N_COL
        grid_col = device_index % N_COL
        block_values = tile_values[grid_row, grid_col].astype(jnp.float32)
        sources = row_blocks[grid_row][tile_rows[grid_row, grid_col]].astype(jnp.float32)
        products = jnp.einsum('kij,kif->kjf', block_values, sources, precision=lax.Precision.HIGHEST)
        active = jnp.arange(SLOTS) < tile_count[grid_row, grid_col]
        onehot = ((tile_cols[grid_row, grid_col][:, None] == jnp.arange(COL_TILES)[None, :]) & active[:, None]).astype(jnp.float32)
        partial_value = jnp.einsum('kg,kjf->gjf', onehot, products, precision=lax.Precision.HIGHEST)
        partial_value = lax.optimization_barrier(partial_value.astype(jnp.bfloat16)).astype(jnp.float32)
        return totals_back.at[grid_col].add(partial_value)
    totals_back = lax.fori_loop(0, N_ROW * N_COL, backward_step, jnp.zeros((N_COL, COL_TILES, TILE, F), jnp.float32))
    grad_hidden = totals_back.reshape(N_COL, N_ROW, ROWS_DEV, F).transpose(1, 0, 2, 3).reshape(NODES, F).astype(jnp.bfloat16)
    grad_features = jnp.dot(grad_hidden, weight.T, preferred_element_type=jnp.float32).astype(jnp.bfloat16)
    grad_weight = jnp.dot(features.T, grad_hidden, preferred_element_type=jnp.float32) * (1.0 / jnp.sqrt(jnp.float32(NODES)))
    return (activated, grad_features, grad_weight)
```

```python
import functools
import math

import jax
import jax.numpy as jnp
from jax import lax
from jax.experimental import pallas as pl
from jax.experimental.pallas import tpu as pltpu
from jax.sharding import PartitionSpec as P

MESH = pl.DeviceIdType.MESH
BF = jnp.bfloat16
F32 = jnp.float32
RIGHT, LEFT = 0, 1


def dot(a, b):
    return jnp.dot(a, b, preferred_element_type=F32)


def kernel(
    dims, feat, weight, vals, tile_rows, tile_cols, tile_count, cot, act_out, gf_out, gw_out,
    gath0, gath1, vt, lhs, picked, own_part, fsend, frecv, ax, slope_v, gblk0, gblk1, tmp, ring_in, sib_in,
    gwf, ga, ar, bs, br, gq, gd, atot,
    ag_s, ag_r, as_s, as_r, fx_s, fx_r, gx_s, gx_r, rs_s, rs_r, rb_s, rb_r,
    a_s, a_r, b_s, b_r, c_s, c_r, d_s, d_r,
):
    n_row, n_col, slots, block, tile, width, per_dev = dims
    chips = n_row // 2
    half = chips // 2
    cut = width // 2
    group = 2 * n_col
    gpart = width // group
    owners = min(chips, gpart // 16)
    prow = gpart // owners
    turns = slots // block
    rows_dev = per_dev * tile
    gath, gblk = (gath0, gath1), (gblk0, gblk1)

    row, col = lax.axis_index("row"), lax.axis_index("col")
    chip, core = row // 2, row % 2
    place = jnp.where(chip % 2 == 0, chip // 2, (2 * chips - 1 - chip) // 2)

    def row_at(position, which):
        position = lax.rem(position + 2 * chips, chips)
        there = jnp.where(position < half, 2 * position, 2 * chips - 1 - 2 * position)
        return there * 2 + which

    ring = ((row_at(place + 1, core), col), (row_at(place - 1, core), col))
    sibling = (chip * 2 + 1 - core, col)
    member = core * n_col + col

    def group_peer(j):
        other = lax.rem(member + j, group)
        return other, (chip * 2 + other // n_col, lax.rem(other, n_col))

    def chip_peer(j):
        other = lax.rem(chip + j, chips)
        return other, (other * 2 + core, col)

    def remote(src, dst, send, recv, device):
        return pltpu.make_async_remote_copy(
            src_ref=src, dst_ref=dst, send_sem=send, recv_sem=recv,
            device_id=device, device_id_type=MESH,
        )

    barrier = pltpu.get_barrier_semaphore()
    for j in range(1, chips):
        pl.semaphore_signal(barrier, inc=1, device_id=chip_peer(j)[1], device_id_type=MESH)
    for j in range(1, group):
        pl.semaphore_signal(barrier, inc=1, device_id=group_peer(j)[1], device_id_type=MESH)
    pl.semaphore_wait(barrier, chips - 1 + group - 1)

    def piece(h, which_row):
        return gath[h].at[pl.ds(which_row * per_dev, per_dev)]

    def columns(h):
        return slice(h * cut, (h + 1) * cut)

    sends = []

    def ag_ring(way, s, h):
        sign = -1 if way == RIGHT else 1
        whose = row_at(place + sign * s, core)
        src = feat.at[:, :, pl.ds(h * cut, cut)] if s == 0 else piece(h, whose)
        return remote(src, piece(h, whose), ag_s.at[way, s, h], ag_r.at[way, s, h], ring[way])

    def ag_sib(offset, h):
        whose = row_at(place + offset, core)
        src = feat.at[:, :, pl.ds(h * cut, cut)] if offset == 0 else piece(h, whose)
        k = offset % chips
        return remote(src, piece(h, whose), as_s.at[k, h], as_r.at[k, h], sibling)

    def used(way, s, h):
        return s < half - 1 or h == way

    for h in range(2):
        for way in (RIGHT, LEFT):
            if used(way, 0, h):
                copy = ag_ring(way, 0, h)
                copy.start()
                sends.append(copy)
    for h in range(2):
        copy = ag_sib(0, h)
        copy.start()
        sends.append(copy)
    for h in range(2):
        gath[h][pl.ds(row * per_dev, per_dev)] = feat[:, :, columns(h)]

    if slots <= 8:
        for k in range(slots):
            vt[k] = vals[k].T
    else:
        @pl.loop(0, slots)
        def _(k):
            vt[k] = vals[k].T

    for s in range(half):
        for h in range(2):
            for way in (RIGHT, LEFT):
                if used(way, s, h):
                    ag_ring(way, s, h).wait_recv()
                    if s + 1 < half and used(way, s + 1, h):
                        copy = ag_ring(way, s + 1, h)
                        copy.start()
                        sends.append(copy)
                    copy = ag_sib((-1 - s) if way == RIGHT else (1 + s), h)
                    copy.start()
                    sends.append(copy)

    live = tile_count[0]

    def fill(source, index, h, turn):
        for k in range(block):
            picked[h, k * tile:(k + 1) * tile, :] = source[h][index[turn * block + k]]

    def product(matrices, index, base, source, source_index, h):
        def one(turn):
            if turns > 1:
                fill(source, source_index, h, turn)
            for k in range(block):
                slot = turn * block + k
                value = matrices[slot]
                for t in range(per_dev):
                    keep = jnp.logical_and(index[slot] == base + t, slot < live)
                    lhs[t * tile:(t + 1) * tile, k * tile:(k + 1) * tile] = lax.select(
                        keep, value, jnp.zeros_like(value)
                    )
            return dot(lhs[...], picked[h])

        if turns == 1:
            return one(0)
        return lax.fori_loop(
            1, turns, lambda turn, total: total + one(turn), one(0)
        )

    def part_copy(h, j):
        to = lax.rem(col + j, n_col)
        return remote(fsend.at[h, j], frecv.at[h, j], fx_s.at[h, j], fx_r.at[h, j], (row, to))

    for h in range(2):
        for offset in range(chips):
            ag_sib(offset, h).wait_recv()
        if turns == 1:
            fill(gath, tile_cols, h, 0)
        for j in range(1, n_col):
            to = lax.rem(col + j, n_col)
            fsend[h, j] = product(vals, tile_rows, to * per_dev, gath, tile_cols, h).astype(BF)
            copy = part_copy(h, j)
            copy.start()
            sends.append(copy)
        own_part[h] = product(vals, tile_rows, col * per_dev, gath, tile_cols, h)

    for copy in sends:
        copy.wait_send()
    sends = []

    summed = None
    for h in range(2):
        for j in range(1, n_col):
            part_copy(h, j).wait_recv()
        total = own_part[h]
        for j in range(1, n_col):
            total = total + frecv[h, j].astype(F32)
        ax[:, columns(h)] = total.astype(BF)
        term = dot(ax[:, columns(h)], weight[columns(h), :])
        summed = term if summed is None else summed + term

    scale = math.sqrt(2.0 / math.pi)
    square = summed * summed
    tanh = jnp.tanh(scale * (summed + 0.044715 * (square * summed)))
    act_out[...] = (0.5 * summed * (1.0 + tanh)).astype(BF)
    steep = 0.5 * (1.0 + tanh) + (0.5 * summed) * (1.0 - tanh * tanh) * (
        scale * (1.0 + (3 * 0.044715) * square)
    )
    slope_v[...] = (cot[...].astype(F32) * steep).astype(BF)

    def slope_copy(h, j):
        to = lax.rem(col + j, n_col)
        mine = gblk[h].at[pl.ds(col * per_dev, per_dev)]
        return remote(mine, mine, gx_s.at[h, j], gx_r.at[h, j], (row, to))

    def from_copy(h, j):
        whose = lax.rem(col - j + n_col, n_col)
        theirs = gblk[h].at[pl.ds(whose * per_dev, per_dev)]
        return remote(theirs, theirs, gx_s.at[h, j], gx_r.at[h, j], (row, lax.rem(col + j, n_col)))

    for h in range(2):
        moved = lax.dot_general(
            slope_v[...], weight[columns(h), :], (((1,), (1,)), ((), ())),
            preferred_element_type=F32,
        ).astype(BF)
        gblk[h][pl.ds(col * per_dev, per_dev)] = moved.reshape(per_dev, tile, cut)
        for j in range(1, n_col):
            copy = slope_copy(h, j)
            copy.start()
            sends.append(copy)

    gwf[...] = lax.dot_general(
        ax[...], slope_v[...], (((0,), (0,)), ((), ())), preferred_element_type=F32
    ).reshape(group, gpart, width)
    ga[...] = gwf[...].astype(BF)

    def a_copy(j):
        other, device = group_peer(j)
        return remote(ga.at[other], ar.at[j], a_s.at[j], a_r.at[j], device)

    def b_copy(j):
        other, device = chip_peer(j)
        return other, remote(
            bs.at[lax.rem(other, owners)], br.at[j], b_s.at[j], b_r.at[j], device
        )

    def c_copy(j, whose):
        _, device = chip_peer(j)
        spot = gq.at[lax.rem(whose, owners)]
        return remote(spot, spot, c_s.at[j], c_r.at[j], device)

    def d_copy(j, whose):
        _, device = group_peer(j)
        return remote(gq, gd.at[whose], d_s.at[j], d_r.at[j], device)

    def when(condition, run):
        if owners == chips:
            run()
        else:
            pl.when(condition)(run)

    def stage_a():
        for j in range(1, group):
            copy = a_copy(j)
            copy.start()

    def stage_b():
        total = gwf[member]
        for j in range(1, group):
            a_copy(j).wait_recv()
            total = total + ar[j].astype(F32)
        atot[...] = total.reshape(owners, prow, width)
        bs[...] = atot[...].astype(BF)
        for j in range(1, chips):
            other, copy = b_copy(j)
            when(other < owners, copy.start)

    def stage_c():
        def reduce():
            total = atot[lax.rem(chip, owners)]
            for j in range(1, chips):
                b_copy(j)[1].wait_recv()
                total = total + br[j].astype(F32)
            node_total = rows_dev * n_row * n_col
            gq[lax.rem(chip, owners)] = (total * (1.0 / math.sqrt(node_total))).astype(BF)
            for j in range(1, chips):
                c_copy(j, chip).start()

        when(chip < owners, reduce)

    def stage_d():
        for j in range(1, chips):
            whose = lax.rem(chip - j + chips, chips)
            when(whose < owners, c_copy(j, whose).wait_recv)
        for j in range(1, group):
            d_copy(j, member).start()

    def finish():
        for j in range(1, group):
            d_copy(j, lax.rem(member - j + group, group)).wait_recv()
            whose = lax.rem(member - j + group, group)
            gw_out[whose] = gd[whose].reshape(gpart, width).astype(F32)
        gw_out[member] = gq[...].reshape(gpart, width).astype(F32)
        for j in range(1, group):
            a_copy(j).wait_send()
            d_copy(j, member).wait_send()
        for j in range(1, chips):
            other, copy = b_copy(j)
            when(other < owners, copy.wait_send)
            when(chip < owners, c_copy(j, chip).wait_send)

    stage_a()

    def term(offset, which, h):
        dest = row_at(place + offset, which)
        return product(vt, tile_cols, dest * per_dev, gblk, tile_rows, h)

    def rb_copy(offset, h):
        k = offset % chips
        return remote(
            piece(h, row_at(place + offset, 1 - core)), sib_in.at[k, h],
            rb_s.at[k, h], rb_r.at[k, h], sibling,
        )

    def rs_copy(way, s, h):
        offset = half - s if way == RIGHT else s - half
        return remote(
            piece(h, row_at(place + offset, core)), ring_in.at[way, s, h],
            rs_s.at[way, s, h], rs_r.at[way, s, h], ring[way],
        )

    def items(s):
        if s == 0:
            return [(RIGHT, 0), (LEFT, 1)]
        if s == half:
            return [(None, 0), (None, 1)]
        return [(RIGHT, 0), (LEFT, 0), (RIGHT, 1), (LEFT, 1)]

    def offset_of(way, s):
        if way is None:
            return 0
        return half - s if way == RIGHT else s - half

    def give(s, way, h):
        offset = offset_of(way, s)
        out = term(offset, 1 - core, h).astype(BF)
        gath[h][pl.ds(row_at(place + offset, 1 - core) * per_dev, per_dev)] = out.reshape(
            per_dev, tile, cut
        )
        copy = rb_copy(offset, h)
        copy.start()
        sends.append(copy)

    def arrive(h):
        for j in range(1, n_col):
            from_copy(h, j).wait_recv()
        if turns == 1:
            fill(gblk, tile_rows, h, 0)

    def came(way, s, h):
        return s > 0 or h == way

    for way, h in items(0):
        arrive(h)
        give(0, way, h)
        tmp[h] = term(offset_of(way, 0), core, h)
    for s in range(half + 1):
        now = items(s)
        if s > 0:
            for n, (way, h) in enumerate(now):
                tmp[n] = term(offset_of(way, s), core, h)
        for n, (way, h) in enumerate(now):
            offset = offset_of(way, s)
            total = tmp[n]
            rb_copy(offset, h).wait_recv()
            total = total + sib_in[offset % chips, h].astype(F32).reshape(rows_dev, cut)
            for source in ((RIGHT, LEFT) if way is None else (way,)):
                if s > 0 and came(source, s - 1, h):
                    rs_copy(source, s - 1, h).wait_recv()
                    total = total + ring_in[source, s - 1, h].astype(F32).reshape(rows_dev, cut)
            if way is None:
                gf_out[:, columns(h)] = total.astype(BF)
            else:
                gath[h][pl.ds(row_at(place + offset, core) * per_dev, per_dev)] = total.astype(
                    BF
                ).reshape(per_dev, tile, cut)
                copy = rs_copy(way, s, h)
                copy.start()
                sends.append(copy)
        if s < half:
            for way, h in items(s + 1):
                give(s + 1, way, h)
        if s == 0:
            stage_b()
        if s == min(1, half - 1):
            stage_c()
        if s == min(2, half - 1):
            stage_d()
    finish()
    for copy in sends:
        copy.wait_send()


def per_device(features, weight, tile_values, tile_rows, tile_cols, tile_count, cotangent):
    rows_dev, width = features.shape
    slots, tile = tile_values.shape[2], tile_values.shape[3]
    n_row, n_col = lax.axis_size("row"), lax.axis_size("col")
    per_dev = rows_dev // tile
    block = min(8, slots)
    chips = n_row // 2
    half = chips // 2
    cut = width // 2
    group = 2 * n_col
    gpart = width // group
    owners = min(chips, gpart // 16)
    prow = gpart // owners
    dims = (n_row, n_col, slots, block, tile, width, per_dev)
    dma = lambda *shape: pltpu.SemaphoreType.DMA(shape)
    vmem = pl.BlockSpec(memory_space=pltpu.VMEM)
    smem = pl.BlockSpec(memory_space=pltpu.SMEM)
    act, gf, gw = pl.pallas_call(
        functools.partial(kernel, dims),
        out_shape=(
            jax.ShapeDtypeStruct((rows_dev, width), BF),
            jax.ShapeDtypeStruct((rows_dev, width), BF),
            jax.ShapeDtypeStruct((group, gpart, width), F32),
        ),
        in_specs=[vmem, vmem, vmem, smem, smem, smem, vmem],
        out_specs=(vmem, vmem, vmem),
        scratch_shapes=[
            pltpu.VMEM((n_row * per_dev, tile, cut), BF),
            pltpu.VMEM((n_row * per_dev, tile, cut), BF),
            pltpu.VMEM((slots, tile, tile), BF),
            pltpu.VMEM((rows_dev, block * tile), BF),
            pltpu.VMEM((2, block * tile, cut), BF),
            pltpu.VMEM((2, rows_dev, cut), F32),
            pltpu.VMEM((2, n_col, rows_dev, cut), BF),
            pltpu.VMEM((2, n_col, rows_dev, cut), BF),
            pltpu.VMEM((rows_dev, width), BF),
            pltpu.VMEM((rows_dev, width), BF),
            pltpu.VMEM((n_col * per_dev, tile, cut), BF),
            pltpu.VMEM((n_col * per_dev, tile, cut), BF),
            pltpu.VMEM((4, rows_dev, cut), F32),
            pltpu.VMEM((2, half, 2, per_dev, tile, cut), BF),
            pltpu.VMEM((chips, 2, per_dev, tile, cut), BF),
            pltpu.VMEM((group, gpart, width), F32),
            pltpu.VMEM((group, gpart, width), BF),
            pltpu.VMEM((group, gpart, width), BF),
            pltpu.VMEM((owners, prow, width), BF),
            pltpu.VMEM((chips, prow, width), BF),
            pltpu.VMEM((owners, prow, width), BF),
            pltpu.VMEM((group, owners, prow, width), BF),
            pltpu.VMEM((owners, prow, width), F32),
            dma(2, half, 2), dma(2, half, 2), dma(chips, 2), dma(chips, 2),
            dma(2, n_col), dma(2, n_col), dma(2, n_col), dma(2, n_col),
            dma(2, half, 2), dma(2, half, 2), dma(chips, 2), dma(chips, 2),
            dma(group), dma(group), dma(chips), dma(chips),
            dma(chips), dma(chips), dma(group), dma(group),
        ],
        compiler_params=pltpu.CompilerParams(
            collective_id=0, has_side_effects=True, vmem_limit_bytes=58 * 1024 * 1024
        ),
        name="graph_layer",
    )(
        features.reshape(per_dev, tile, width),
        weight,
        tile_values[0, 0],
        tile_rows[0, 0],
        tile_cols[0, 0],
        tile_count[0],
        cotangent,
    )
    return act, gf, gw.reshape(width, width)


def solution(mesh):
    in_specs = (
        P(("row", "col"), None),
        P(),
        P("row", "col", None, None, None),
        P("row", "col", None),
        P("row", "col", None),
        P("row", "col"),
        P(("row", "col"), None),
    )
    out_specs = (P(("row", "col"), None), P(("row", "col"), None), P())
    return jax.shard_map(
        per_device, mesh=mesh, in_specs=in_specs, out_specs=out_specs, check_vma=False
    )
```

```python
import functools
import math

import jax
import jax.numpy as jnp
from jax import lax
from jax.experimental import pallas as pl
from jax.experimental.pallas import tpu as pltpu
from jax.sharding import PartitionSpec as P

MESH = pl.DeviceIdType.MESH
BF = jnp.bfloat16
F32 = jnp.float32
RIGHT, LEFT = 0, 1


def dot(a, b):
    return jnp.dot(a, b, preferred_element_type=F32)


def kernel(
    dims, feat, weight, vals, tile_rows, tile_cols, tile_count, cot, act_out, gf_out, gw_out,
    gath0, gath1, vt, lhs, picked, own_part, fsend, frecv, ax, slope_v, gblk0, gblk1, tmp, ring_in, sib_in,
    gwf, ga, ar, bs, br, gq, gd, atot,
    ag_s, ag_r, as_s, as_r, fx_s, fx_r, gx_s, gx_r, rs_s, rs_r, rb_s, rb_r,
    a_s, a_r, b_s, b_r, c_s, c_r, d_s, d_r,
):
    n_row, n_col, slots, block, tile, width, per_dev = dims
    chips = n_row // 2
    half = chips // 2
    cut = width // 2
    group = 2 * n_col
    gpart = width // group
    owners = min(chips, gpart // 16)
    prow = gpart // owners
    turns = slots // block
    rows_dev = per_dev * tile
    gath, gblk = (gath0, gath1), (gblk0, gblk1)

    row, col = lax.axis_index("row"), lax.axis_index("col")
    chip, core = row // 2, row % 2
    place = jnp.where(chip % 2 == 0, chip // 2, (2 * chips - 1 - chip) // 2)

    def row_at(position, which):
        position = lax.rem(position + 2 * chips, chips)
        there = jnp.where(position < half, 2 * position, 2 * chips - 1 - 2 * position)
        return there * 2 + which

    ring = ((row_at(place + 1, core), col), (row_at(place - 1, core), col))
    sibling = (chip * 2 + 1 - core, col)
    member = core * n_col + col

    def group_peer(j):
        other = lax.rem(member + j, group)
        return other, (chip * 2 + other // n_col, lax.rem(other, n_col))

    def chip_peer(j):
        other = lax.rem(chip + j, chips)
        return other, (other * 2 + core, col)

    def remote(src, dst, send, recv, device):
        return pltpu.make_async_remote_copy(
            src_ref=src, dst_ref=dst, send_sem=send, recv_sem=recv,
            device_id=device, device_id_type=MESH,
        )

    barrier = pltpu.get_barrier_semaphore()
    for j in range(1, chips):
        pl.semaphore_signal(barrier, inc=1, device_id=chip_peer(j)[1], device_id_type=MESH)
    for j in range(1, group):
        pl.semaphore_signal(barrier, inc=1, device_id=group_peer(j)[1], device_id_type=MESH)
    pl.semaphore_wait(barrier, chips - 1 + group - 1)

    def piece(h, which_row):
        return gath[h].at[pl.ds(which_row * per_dev, per_dev)]

    def columns(h):
        return slice(h * cut, (h + 1) * cut)

    sends = []

    def ag_ring(way, s, h, t):
        sign = -1 if way == RIGHT else 1
        whose = row_at(place + sign * s, core)
        dst = gath[h].at[whose * per_dev + t]
        src = feat.at[t, :, pl.ds(h * cut, cut)] if s == 0 else dst
        return remote(src, dst, ag_s.at[way, s, h, t], ag_r.at[way, s, h, t], ring[way])

    def ag_sib(offset, h):
        whose = row_at(place + offset, core)
        src = feat.at[:, :, pl.ds(h * cut, cut)] if offset == 0 else piece(h, whose)
        k = offset % chips
        return remote(src, piece(h, whose), as_s.at[k, h], as_r.at[k, h], sibling)

    def used(way, s, h):
        return s < half - 1 or h == way

    def ag_start(way, s, h, t):
        copy = ag_ring(way, s, h, t)
        copy.start()
        sends.append(copy)

    for t in range(per_dev):
        for way in (RIGHT, LEFT):
            ag_start(way, 0, 0, t)
    for h in range(2):
        copy = ag_sib(0, h)
        copy.start()
        sends.append(copy)
    for h in range(2):
        gath[h][pl.ds(row * per_dev, per_dev)] = feat[:, :, columns(h)]

    if slots <= 8:
        for k in range(slots):
            vt[k] = vals[k].T
    else:
        @pl.loop(0, slots)
        def _(k):
            vt[k] = vals[k].T

    live = tile_count[0]

    def fill(source, index, h, turn):
        for k in range(block):
            picked[h, k * tile:(k + 1) * tile, :] = source[h][index[turn * block + k]]

    def product(matrices, index, base, source, source_index, h):
        def one(turn):
            if turns > 1:
                fill(source, source_index, h, turn)
            for k in range(block):
                slot = turn * block + k
                value = matrices[slot]
                for t in range(per_dev):
                    keep = jnp.logical_and(index[slot] == base + t, slot < live)
                    lhs[t * tile:(t + 1) * tile, k * tile:(k + 1) * tile] = lax.select(
                        keep, value, jnp.zeros_like(value)
                    )
            return dot(lhs[...], picked[h])

        if turns == 1:
            return one(0)
        return lax.fori_loop(
            1, turns, lambda turn, total: total + one(turn), one(0)
        )

    def part_copy(h, j):
        to = lax.rem(col + j, n_col)
        return remote(fsend.at[h, j], frecv.at[h, j], fx_s.at[h, j], fx_r.at[h, j], (row, to))

    def forward(h):
        for offset in range(chips):
            ag_sib(offset, h).wait_recv()
        if turns == 1:
            fill(gath, tile_cols, h, 0)
        for j in range(1, n_col):
            to = lax.rem(col + j, n_col)
            fsend[h, j] = product(vals, tile_rows, to * per_dev, gath, tile_cols, h).astype(BF)
            copy = part_copy(h, j)
            copy.start()
            sends.append(copy)
        own_part[h] = product(vals, tile_rows, col * per_dev, gath, tile_cols, h)

    for h in range(2):
        for s in range(half):
            for t in range(per_dev):
                for way in (RIGHT, LEFT):
                    if used(way, s, h):
                        ag_ring(way, s, h, t).wait_recv()
                        if s + 1 < half and used(way, s + 1, h):
                            ag_start(way, s + 1, h, t)
            for way in (RIGHT, LEFT):
                if h == 0 and used(way, s, h) and not (s + 2 < half and used(way, s + 2, h)):
                    if s + 1 < half and used(way, s + 1, h):
                        for t in range(per_dev):
                            ag_start(way, 0, 1, t)
                if used(way, s, h):
                    copy = ag_sib((-1 - s) if way == RIGHT else (1 + s), h)
                    copy.start()
                    sends.append(copy)
            if h == 1 and s == 0:
                forward(0)
    forward(1)

    for copy in sends:
        copy.wait_send()
    sends = []

    summed = None
    for h in range(2):
        for j in range(1, n_col):
            part_copy(h, j).wait_recv()
        total = own_part[h]
        for j in range(1, n_col):
            total = total + frecv[h, j].astype(F32)
        ax[:, columns(h)] = total.astype(BF)
        term = dot(ax[:, columns(h)], weight[columns(h), :])
        summed = term if summed is None else summed + term

    scale = math.sqrt(2.0 / math.pi)
    square = summed * summed
    tanh = jnp.tanh(scale * (summed + 0.044715 * (square * summed)))
    act_out[...] = (0.5 * summed * (1.0 + tanh)).astype(BF)
    steep = 0.5 * (1.0 + tanh) + (0.5 * summed) * (1.0 - tanh * tanh) * (
        scale * (1.0 + (3 * 0.044715) * square)
    )
    slope_v[...] = (cot[...].astype(F32) * steep).astype(BF)

    def slope_copy(h, j):
        to = lax.rem(col + j, n_col)
        mine = gblk[h].at[pl.ds(col * per_dev, per_dev)]
        return remote(mine, mine, gx_s.at[h, j], gx_r.at[h, j], (row, to))

    def from_copy(h, j):
        whose = lax.rem(col - j + n_col, n_col)
        theirs = gblk[h].at[pl.ds(whose * per_dev, per_dev)]
        return remote(theirs, theirs, gx_s.at[h, j], gx_r.at[h, j], (row, lax.rem(col + j, n_col)))

    for h in range(2):
        moved = lax.dot_general(
            slope_v[...], weight[columns(h), :], (((1,), (1,)), ((), ())),
            preferred_element_type=F32,
        ).astype(BF)
        gblk[h][pl.ds(col * per_dev, per_dev)] = moved.reshape(per_dev, tile, cut)
        for j in range(1, n_col):
            copy = slope_copy(h, j)
            copy.start()
            sends.append(copy)

    def a_copy(j):
        other, device = group_peer(j)
        return remote(ga.at[other], ar.at[j], a_s.at[j], a_r.at[j], device)

    def b_copy(j):
        other, device = chip_peer(j)
        return other, remote(
            bs.at[lax.rem(other, owners)], br.at[j], b_s.at[j], b_r.at[j], device
        )

    def c_copy(j, whose):
        _, device = chip_peer(j)
        spot = gq.at[lax.rem(whose, owners)]
        return remote(spot, spot, c_s.at[j], c_r.at[j], device)

    def d_copy(j, whose):
        _, device = group_peer(j)
        return remote(gq, gd.at[whose], d_s.at[j], d_r.at[j], device)

    def when(condition, run):
        if owners == chips:
            run()
        else:
            pl.when(condition)(run)

    def stage_a():
        gwf[...] = lax.dot_general(
            ax[...], slope_v[...], (((0,), (0,)), ((), ())), preferred_element_type=F32
        ).reshape(group, gpart, width)
        ga[...] = gwf[...].astype(BF)
        for j in range(1, group):
            copy = a_copy(j)
            copy.start()

    def stage_b():
        total = gwf[member]
        for j in range(1, group):
            a_copy(j).wait_recv()
            total = total + ar[j].astype(F32)
        atot[...] = total.reshape(owners, prow, width)
        bs[...] = atot[...].astype(BF)
        for j in range(1, chips):
            other, copy = b_copy(j)
            when(other < owners, copy.start)

    def stage_c():
        def reduce():
            total = atot[lax.rem(chip, owners)]
            for j in range(1, chips):
                b_copy(j)[1].wait_recv()
                total = total + br[j].astype(F32)
            node_total = rows_dev * n_row * n_col
            gq[lax.rem(chip, owners)] = (total * (1.0 / math.sqrt(node_total))).astype(BF)
            for j in range(1, chips):
                c_copy(j, chip).start()

        when(chip < owners, reduce)

    def stage_d():
        for j in range(1, chips):
            whose = lax.rem(chip - j + chips, chips)
            when(whose < owners, c_copy(j, whose).wait_recv)
        for j in range(1, group):
            d_copy(j, member).start()

    def finish():
        for j in range(1, group):
            d_copy(j, lax.rem(member - j + group, group)).wait_recv()
            whose = lax.rem(member - j + group, group)
            gw_out[whose] = gd[whose].reshape(gpart, width)
        gw_out[member] = gq[...].reshape(gpart, width)
        for j in range(1, group):
            a_copy(j).wait_send()
            d_copy(j, member).wait_send()
        for j in range(1, chips):
            other, copy = b_copy(j)
            when(other < owners, copy.wait_send)
            when(chip < owners, c_copy(j, chip).wait_send)

    def term(offset, which, h):
        dest = row_at(place + offset, which)
        return product(vt, tile_cols, dest * per_dev, gblk, tile_rows, h)

    def rb_copy(offset, h):
        k = offset % chips
        return remote(
            piece(h, row_at(place + offset, 1 - core)), sib_in.at[k, h],
            rb_s.at[k, h], rb_r.at[k, h], sibling,
        )

    def rs_copy(way, s, h, t):
        offset = half - s if way == RIGHT else s - half
        return remote(
            gath[h].at[row_at(place + offset, core) * per_dev + t], ring_in.at[way, s, h, t],
            rs_s.at[way, s, h, t], rs_r.at[way, s, h, t], ring[way],
        )

    def items(s, h):
        if s == 0:
            return [(RIGHT, LEFT)[h]]
        return [None] if s == half else [RIGHT, LEFT]

    def offset_of(way, s):
        if way is None:
            return 0
        return half - s if way == RIGHT else s - half

    def give(s, way, h):
        offset = offset_of(way, s)
        out = term(offset, 1 - core, h).astype(BF)
        gath[h][pl.ds(row_at(place + offset, 1 - core) * per_dev, per_dev)] = out.reshape(
            per_dev, tile, cut
        )
        copy = rb_copy(offset, h)
        copy.start()
        sends.append(copy)

    def arrive(h):
        for j in range(1, n_col):
            from_copy(h, j).wait_recv()
        if turns == 1:
            fill(gblk, tile_rows, h, 0)

    def came(way, s, h):
        return s > 0 or h == way

    order = [(0, 0), (1, 0), (0, 1)] + [(s, 0) for s in range(2, half)]
    order += [(1, 1), (half, 0)] + [(s, 1) for s in range(2, half + 1)]
    stages = {0: stage_a, 2: stage_b, 4: stage_c, 6: stage_d}

    def give_all(n):
        s, h = order[n]
        if s == 0:
            arrive(h)
        for way in items(s, h):
            give(s, way, h)

    give_all(0)
    for n, (s, h) in enumerate(order):
        for m, way in enumerate(items(s, h)):
            tmp[m] = term(offset_of(way, s), core, h)
        for m, way in enumerate(items(s, h)):
            offset = offset_of(way, s)
            rb_copy(offset, h).wait_recv()
            tmp[m] += sib_in[offset % chips, h].astype(F32).reshape(rows_dev, cut)
        for t in range(per_dev):
            rows = slice(t * tile, (t + 1) * tile)
            for m, way in enumerate(items(s, h)):
                total = tmp[m, rows]
                for source in ((RIGHT, LEFT) if way is None else (way,)):
                    if s > 0 and came(source, s - 1, h):
                        rs_copy(source, s - 1, h, t).wait_recv()
                        total = total + ring_in[source, s - 1, h, t].astype(F32)
                if way is None:
                    gf_out[rows, columns(h)] = total.astype(BF)
                else:
                    dest = row_at(place + offset_of(way, s), core)
                    gath[h][dest * per_dev + t] = total.astype(BF)
                    copy = rs_copy(way, s, h, t)
                    copy.start()
                    sends.append(copy)
        if n + 1 < len(order):
            give_all(n + 1)
        if n in stages:
            stages[n]()
    finish()
    for copy in sends:
        copy.wait_send()


def write(act, gf, gw, act_out, gf_out, gw_out):
    act_out[...] = act[...]
    gf_out[...] = gf[...]
    gw_out[...] = gw[...].astype(F32)


def per_device(features, weight, tile_values, tile_rows, tile_cols, tile_count, cotangent):
    rows_dev, width = features.shape
    slots, tile = tile_values.shape[2], tile_values.shape[3]
    n_row, n_col = lax.axis_size("row"), lax.axis_size("col")
    per_dev = rows_dev // tile
    block = min(8, slots)
    chips = n_row // 2
    half = chips // 2
    cut = width // 2
    group = 2 * n_col
    gpart = width // group
    owners = min(chips, gpart // 16)
    prow = gpart // owners
    dims = (n_row, n_col, slots, block, tile, width, per_dev)
    dma = lambda *shape: pltpu.SemaphoreType.DMA(shape)
    vmem = pl.BlockSpec(memory_space=pltpu.VMEM)
    smem = pl.BlockSpec(memory_space=pltpu.SMEM)
    act, gf, gw = pl.pallas_call(
        functools.partial(kernel, dims),
        out_shape=(
            jax.ShapeDtypeStruct((rows_dev, width), BF),
            jax.ShapeDtypeStruct((rows_dev, width), BF),
            jax.ShapeDtypeStruct((group, gpart, width), BF),
        ),
        in_specs=[vmem, vmem, vmem, smem, smem, smem, vmem],
        out_specs=(vmem, vmem, vmem),
        scratch_shapes=[
            pltpu.VMEM((n_row * per_dev, tile, cut), BF),
            pltpu.VMEM((n_row * per_dev, tile, cut), BF),
            pltpu.VMEM((slots, tile, tile), BF),
            pltpu.VMEM((rows_dev, block * tile), BF),
            pltpu.VMEM((2, block * tile, cut), BF),
            pltpu.VMEM((2, rows_dev, cut), F32),
            pltpu.VMEM((2, n_col, rows_dev, cut), BF),
            pltpu.VMEM((2, n_col, rows_dev, cut), BF),
            pltpu.VMEM((rows_dev, width), BF),
            pltpu.VMEM((rows_dev, width), BF),
            pltpu.VMEM((n_col * per_dev, tile, cut), BF),
            pltpu.VMEM((n_col * per_dev, tile, cut), BF),
            pltpu.VMEM((4, rows_dev, cut), F32),
            pltpu.VMEM((2, half, 2, per_dev, tile, cut), BF),
            pltpu.VMEM((chips, 2, per_dev, tile, cut), BF),
            pltpu.VMEM((group, gpart, width), F32),
            pltpu.VMEM((group, gpart, width), BF),
            pltpu.VMEM((group, gpart, width), BF),
            pltpu.VMEM((owners, prow, width), BF),
            pltpu.VMEM((chips, prow, width), BF),
            pltpu.VMEM((owners, prow, width), BF),
            pltpu.VMEM((group, owners, prow, width), BF),
            pltpu.VMEM((owners, prow, width), F32),
            dma(2, half, 2, per_dev), dma(2, half, 2, per_dev), dma(chips, 2), dma(chips, 2),
            dma(2, n_col), dma(2, n_col), dma(2, n_col), dma(2, n_col),
            dma(2, half, 2, per_dev), dma(2, half, 2, per_dev), dma(chips, 2), dma(chips, 2),
            dma(group), dma(group), dma(chips), dma(chips),
            dma(chips), dma(chips), dma(group), dma(group),
        ],
        compiler_params=pltpu.CompilerParams(
            collective_id=0, has_side_effects=True, vmem_limit_bytes=58 * 1024 * 1024
        ),
        name="graph_layer",
    )(
        features.reshape(per_dev, tile, width),
        weight,
        tile_values[0, 0],
        tile_rows[0, 0],
        tile_cols[0, 0],
        tile_count[0],
        cotangent,
    )
    return pl.pallas_call(
        write,
        out_shape=(
            jax.ShapeDtypeStruct((rows_dev, width), BF),
            jax.ShapeDtypeStruct((rows_dev, width), BF),
            jax.ShapeDtypeStruct((width, width), F32),
        ),
        in_specs=[vmem, vmem, vmem],
        out_specs=(vmem, vmem, vmem),
        name="write",
    )(act, gf, gw.reshape(width, width))


def solution(mesh):
    in_specs = (
        P(("row", "col"), None),
        P(),
        P("row", "col", None, None, None),
        P("row", "col", None),
        P("row", "col", None),
        P("row", "col"),
        P(("row", "col"), None),
    )
    out_specs = (P(("row", "col"), None), P(("row", "col"), None), P())
    return jax.shard_map(
        per_device, mesh=mesh, in_specs=in_specs, out_specs=out_specs, check_vma=False
    )
```

```python
import functools
import math

import jax
import jax.numpy as jnp
from jax import lax
from jax.experimental import pallas as pl
from jax.experimental.pallas import tpu as pltpu
from jax.sharding import PartitionSpec as P

MESH = pl.DeviceIdType.MESH
BF = jnp.bfloat16
F32 = jnp.float32
RIGHT, LEFT = 0, 1


def dot(a, b):
    return jnp.dot(a, b, preferred_element_type=F32)


def kernel(
    dims, feat, weight, vals, tile_rows, tile_cols, tile_count, cot, act_out, gf_out, gw_out,
    gath0, gath1, vt, lhs, picked, own_part, fsend, frecv, ax, slope_v, gblk0, gblk1, tmp, ring_in, sib_in,
    gwf, ga, ar, bs, br, gq, gd, atot,
    ag_s, ag_r, as_s, as_r, fx_s, fx_r, gx_s, gx_r, rs_s, rs_r, rb_s, rb_r,
    a_s, a_r, b_s, b_r, c_s, c_r, d_s, d_r,
):
    n_row, n_col, slots, block, tile, width, per_dev = dims
    chips = n_row // 2
    half = chips // 2
    cut = width // 2
    group = 2 * n_col
    gpart = width // group
    owners = min(chips, gpart // 16)
    prow = gpart // owners
    turns = slots // block
    rows_dev = per_dev * tile
    gath, gblk = (gath0, gath1), (gblk0, gblk1)

    row, col = lax.axis_index("row"), lax.axis_index("col")
    chip, core = row // 2, row % 2
    place = jnp.where(chip % 2 == 0, chip // 2, (2 * chips - 1 - chip) // 2)

    def row_at(position, which):
        position = lax.rem(position + 2 * chips, chips)
        there = jnp.where(position < half, 2 * position, 2 * chips - 1 - 2 * position)
        return there * 2 + which

    ring = ((row_at(place + 1, core), col), (row_at(place - 1, core), col))
    sibling = (chip * 2 + 1 - core, col)
    member = core * n_col + col

    def group_peer(j):
        other = lax.rem(member + j, group)
        return other, (chip * 2 + other // n_col, lax.rem(other, n_col))

    def chip_peer(j):
        other = lax.rem(chip + j, chips)
        return other, (other * 2 + core, col)

    def remote(src, dst, send, recv, device):
        return pltpu.make_async_remote_copy(
            src_ref=src, dst_ref=dst, send_sem=send, recv_sem=recv,
            device_id=device, device_id_type=MESH,
        )

    barrier = pltpu.get_barrier_semaphore()
    for j in range(1, chips):
        pl.semaphore_signal(barrier, inc=1, device_id=chip_peer(j)[1], device_id_type=MESH)
    for j in range(1, group):
        pl.semaphore_signal(barrier, inc=1, device_id=group_peer(j)[1], device_id_type=MESH)
    pl.semaphore_wait(barrier, chips - 1 + group - 1)

    def piece(h, which_row):
        return gath[h].at[pl.ds(which_row * per_dev, per_dev)]

    def columns(h):
        return slice(h * cut, (h + 1) * cut)

    sends = []

    def ag_ring(way, s, h, t):
        sign = -1 if way == RIGHT else 1
        whose = row_at(place + sign * s, core)
        dst = gath[h].at[whose * per_dev + t]
        src = feat.at[t, :, pl.ds(h * cut, cut)] if s == 0 else dst
        return remote(src, dst, ag_s.at[way, s, h, t], ag_r.at[way, s, h, t], ring[way])

    def ag_sib(offset, h):
        whose = row_at(place + offset, core)
        src = feat.at[:, :, pl.ds(h * cut, cut)] if offset == 0 else piece(h, whose)
        k = offset % chips
        return remote(src, piece(h, whose), as_s.at[k, h], as_r.at[k, h], sibling)

    def used(way, s, h):
        return s < half - 1 or h == way

    def ag_start(way, s, h, t):
        copy = ag_ring(way, s, h, t)
        copy.start()
        sends.append(copy)

    for t in range(per_dev):
        for way in (RIGHT, LEFT):
            ag_start(way, 0, 0, t)
    for h in range(2):
        copy = ag_sib(0, h)
        copy.start()
        sends.append(copy)
    for h in range(2):
        gath[h][pl.ds(row * per_dev, per_dev)] = feat[:, :, columns(h)]

    if slots <= 8:
        for k in range(slots):
            vt[k] = vals[k].T
    else:
        @pl.loop(0, slots)
        def _(k):
            vt[k] = vals[k].T

    live = tile_count[0]

    def fill(source, index, h, turn):
        for k in range(block):
            picked[h, k * tile:(k + 1) * tile, :] = source[h][index[turn * block + k]]

    def product(matrices, index, base, source, source_index, h):
        def one(turn):
            if turns > 1:
                fill(source, source_index, h, turn)
            for k in range(block):
                slot = turn * block + k
                value = matrices[slot]
                for t in range(per_dev):
                    keep = jnp.logical_and(index[slot] == base + t, slot < live)
                    lhs[t * tile:(t + 1) * tile, k * tile:(k + 1) * tile] = lax.select(
                        keep, value, jnp.zeros_like(value)
                    )
            return dot(lhs[...], picked[h])

        if turns == 1:
            return one(0)
        return lax.fori_loop(
            1, turns, lambda turn, total: total + one(turn), one(0)
        )

    def part_copy(h, j):
        to = lax.rem(col + j, n_col)
        return remote(fsend.at[h, j], frecv.at[h, j], fx_s.at[h, j], fx_r.at[h, j], (row, to))

    def forward(h):
        for offset in range(chips):
            ag_sib(offset, h).wait_recv()
        if turns == 1:
            fill(gath, tile_cols, h, 0)
        for j in range(1, n_col):
            to = lax.rem(col + j, n_col)
            fsend[h, j] = product(vals, tile_rows, to * per_dev, gath, tile_cols, h).astype(BF)
            copy = part_copy(h, j)
            copy.start()
            sends.append(copy)
        own_part[h] = product(vals, tile_rows, col * per_dev, gath, tile_cols, h)

    for h in range(2):
        for s in range(half):
            for t in range(per_dev):
                for way in (RIGHT, LEFT):
                    if used(way, s, h):
                        ag_ring(way, s, h, t).wait_recv()
                        if s + 1 < half and used(way, s + 1, h):
                            ag_start(way, s + 1, h, t)
            for way in (RIGHT, LEFT):
                if h == 0 and used(way, s, h) and not (s + 2 < half and used(way, s + 2, h)):
                    if s + 1 < half and used(way, s + 1, h):
                        for t in range(per_dev):
                            ag_start(way, 0, 1, t)
                if used(way, s, h):
                    copy = ag_sib((-1 - s) if way == RIGHT else (1 + s), h)
                    copy.start()
                    sends.append(copy)
            if h == 1 and s == 0:
                forward(0)
    forward(1)

    for copy in sends:
        copy.wait_send()
    sends = []

    summed = None
    for h in range(2):
        for j in range(1, n_col):
            part_copy(h, j).wait_recv()
        total = own_part[h]
        for j in range(1, n_col):
            total = total + frecv[h, j].astype(F32)
        ax[:, columns(h)] = total.astype(BF)
        term = dot(ax[:, columns(h)], weight[columns(h), :])
        summed = term if summed is None else summed + term

    scale = math.sqrt(2.0 / math.pi)
    square = summed * summed
    tanh = jnp.tanh(scale * (summed + 0.044715 * (square * summed)))
    act_out[...] = (0.5 * summed * (1.0 + tanh)).astype(BF)
    steep = 0.5 * (1.0 + tanh) + (0.5 * summed) * (1.0 - tanh * tanh) * (
        scale * (1.0 + (3 * 0.044715) * square)
    )
    slope_v[...] = (cot[...].astype(F32) * steep).astype(BF)

    def slope_copy(h, j):
        to = lax.rem(col + j, n_col)
        mine = gblk[h].at[pl.ds(col * per_dev, per_dev)]
        return remote(mine, mine, gx_s.at[h, j], gx_r.at[h, j], (row, to))

    def from_copy(h, j):
        whose = lax.rem(col - j + n_col, n_col)
        theirs = gblk[h].at[pl.ds(whose * per_dev, per_dev)]
        return remote(theirs, theirs, gx_s.at[h, j], gx_r.at[h, j], (row, lax.rem(col + j, n_col)))

    for h in range(2):
        moved = lax.dot_general(
            slope_v[...], weight[columns(h), :], (((1,), (1,)), ((), ())),
            preferred_element_type=F32,
        ).astype(BF)
        gblk[h][pl.ds(col * per_dev, per_dev)] = moved.reshape(per_dev, tile, cut)
        for j in range(1, n_col):
            copy = slope_copy(h, j)
            copy.start()
            sends.append(copy)

    def a_copy(j):
        other, device = group_peer(j)
        return remote(ga.at[other], ar.at[j], a_s.at[j], a_r.at[j], device)

    def b_copy(j):
        other, device = chip_peer(j)
        return other, remote(
            bs.at[lax.rem(other, owners)], br.at[j], b_s.at[j], b_r.at[j], device
        )

    def c_copy(j, whose):
        _, device = chip_peer(j)
        spot = gq.at[lax.rem(whose, owners)]
        return remote(spot, spot, c_s.at[j], c_r.at[j], device)

    def d_copy(j, whose):
        _, device = group_peer(j)
        return remote(gq, gd.at[whose], d_s.at[j], d_r.at[j], device)

    def when(condition, run):
        if owners == chips:
            run()
        else:
            pl.when(condition)(run)

    def stage_a():
        gwf[...] = lax.dot_general(
            ax[...], slope_v[...], (((0,), (0,)), ((), ())), preferred_element_type=F32
        ).reshape(group, gpart, width)
        ga[...] = gwf[...].astype(BF)
        for j in range(1, group):
            copy = a_copy(j)
            copy.start()

    def stage_b():
        total = gwf[member]
        for j in range(1, group):
            a_copy(j).wait_recv()
            total = total + ar[j].astype(F32)
        atot[...] = total.reshape(owners, prow, width)
        bs[...] = atot[...].astype(BF)
        for j in range(1, chips):
            other, copy = b_copy(j)
            when(other < owners, copy.start)

    def stage_c():
        def reduce():
            total = atot[lax.rem(chip, owners)]
            for j in range(1, chips):
                b_copy(j)[1].wait_recv()
                total = total + br[j].astype(F32)
            node_total = rows_dev * n_row * n_col
            gq[lax.rem(chip, owners)] = (total * (1.0 / math.sqrt(node_total))).astype(BF)
            for j in range(1, chips):
                c_copy(j, chip).start()

        when(chip < owners, reduce)

    def stage_d():
        for j in range(1, chips):
            whose = lax.rem(chip - j + chips, chips)
            when(whose < owners, c_copy(j, whose).wait_recv)
        for j in range(1, group):
            d_copy(j, member).start()

    def finish():
        for j in range(1, group):
            d_copy(j, lax.rem(member - j + group, group)).wait_recv()
            whose = lax.rem(member - j + group, group)
            gw_out[whose] = gd[whose].reshape(gpart, width)
        gw_out[member] = gq[...].reshape(gpart, width)
        for j in range(1, group):
            a_copy(j).wait_send()
            d_copy(j, member).wait_send()
        for j in range(1, chips):
            other, copy = b_copy(j)
            when(other < owners, copy.wait_send)
            when(chip < owners, c_copy(j, chip).wait_send)

    def term(offset, which, h):
        dest = row_at(place + offset, which)
        return product(vt, tile_cols, dest * per_dev, gblk, tile_rows, h)

    def rb_copy(offset, h):
        k = offset % chips
        return remote(
            piece(h, row_at(place + offset, 1 - core)), sib_in.at[k, h],
            rb_s.at[k, h], rb_r.at[k, h], sibling,
        )

    def rs_copy(way, s, h, t):
        offset = half - s if way == RIGHT else s - half
        return remote(
            gath[h].at[row_at(place + offset, core) * per_dev + t], ring_in.at[way, s, h, t],
            rs_s.at[way, s, h, t], rs_r.at[way, s, h, t], ring[way],
        )

    def items(s, h):
        if s == 0:
            return [(RIGHT, LEFT)[h]]
        return [None] if s == half else [RIGHT, LEFT]

    def offset_of(way, s):
        if way is None:
            return 0
        return half - s if way == RIGHT else s - half

    def give(s, way, h):
        offset = offset_of(way, s)
        out = term(offset, 1 - core, h).astype(BF)
        gath[h][pl.ds(row_at(place + offset, 1 - core) * per_dev, per_dev)] = out.reshape(
            per_dev, tile, cut
        )
        copy = rb_copy(offset, h)
        copy.start()
        sends.append(copy)

    def arrive(h):
        for j in range(1, n_col):
            from_copy(h, j).wait_recv()
        if turns == 1:
            fill(gblk, tile_rows, h, 0)

    def came(way, s, h):
        return s > 0 or h == way

    order = [(s, h) for s in range(half + 1) for h in range(2)]
    stages = {0: stage_a, 2: stage_b, 4: stage_c, 6: stage_d}

    def give_all(n):
        s, h = order[n]
        if s == 0:
            arrive(h)
        for way in items(s, h):
            give(s, way, h)

    give_all(0)
    for n, (s, h) in enumerate(order):
        for m, way in enumerate(items(s, h)):
            tmp[m] = term(offset_of(way, s), core, h)
        for m, way in enumerate(items(s, h)):
            offset = offset_of(way, s)
            rb_copy(offset, h).wait_recv()
            tmp[m] += sib_in[offset % chips, h].astype(F32).reshape(rows_dev, cut)
        for t in range(per_dev):
            rows = slice(t * tile, (t + 1) * tile)
            for m, way in enumerate(items(s, h)):
                total = tmp[m, rows]
                for source in ((RIGHT, LEFT) if way is None else (way,)):
                    if s > 0 and came(source, s - 1, h):
                        rs_copy(source, s - 1, h, t).wait_recv()
                        total = total + ring_in[source, s - 1, h, t].astype(F32)
                if way is None:
                    gf_out[rows, columns(h)] = total.astype(BF)
                else:
                    dest = row_at(place + offset_of(way, s), core)
                    gath[h][dest * per_dev + t] = total.astype(BF)
                    copy = rs_copy(way, s, h, t)
                    copy.start()
                    sends.append(copy)
        if n + 1 < len(order):
            give_all(n + 1)
        if n in stages:
            stages[n]()
    finish()
    for copy in sends:
        copy.wait_send()


def write(act, gf, gw, act_out, gf_out, gw_out):
    act_out[...] = act[...]
    gf_out[...] = gf[...]
    gw_out[...] = gw[...].astype(F32)


def per_device(features, weight, tile_values, tile_rows, tile_cols, tile_count, cotangent):
    rows_dev, width = features.shape
    slots, tile = tile_values.shape[2], tile_values.shape[3]
    n_row, n_col = lax.axis_size("row"), lax.axis_size("col")
    per_dev = rows_dev // tile
    block = min(8, slots)
    chips = n_row // 2
    half = chips // 2
    cut = width // 2
    group = 2 * n_col
    gpart = width // group
    owners = min(chips, gpart // 16)
    prow = gpart // owners
    dims = (n_row, n_col, slots, block, tile, width, per_dev)
    dma = lambda *shape: pltpu.SemaphoreType.DMA(shape)
    vmem = pl.BlockSpec(memory_space=pltpu.VMEM)
    smem = pl.BlockSpec(memory_space=pltpu.SMEM)
    act, gf, gw = pl.pallas_call(
        functools.partial(kernel, dims),
        out_shape=(
            jax.ShapeDtypeStruct((rows_dev, width), BF),
            jax.ShapeDtypeStruct((rows_dev, width), BF),
            jax.ShapeDtypeStruct((group, gpart, width), BF),
        ),
        in_specs=[vmem, vmem, vmem, smem, smem, smem, vmem],
        out_specs=(vmem, vmem, vmem),
        scratch_shapes=[
            pltpu.VMEM((n_row * per_dev, tile, cut), BF),
            pltpu.VMEM((n_row * per_dev, tile, cut), BF),
            pltpu.VMEM((slots, tile, tile), BF),
            pltpu.VMEM((rows_dev, block * tile), BF),
            pltpu.VMEM((2, block * tile, cut), BF),
            pltpu.VMEM((2, rows_dev, cut), F32),
            pltpu.VMEM((2, n_col, rows_dev, cut), BF),
            pltpu.VMEM((2, n_col, rows_dev, cut), BF),
            pltpu.VMEM((rows_dev, width), BF),
            pltpu.VMEM((rows_dev, width), BF),
            pltpu.VMEM((n_col * per_dev, tile, cut), BF),
            pltpu.VMEM((n_col * per_dev, tile, cut), BF),
            pltpu.VMEM((4, rows_dev, cut), F32),
            pltpu.VMEM((2, half, 2, per_dev, tile, cut), BF),
            pltpu.VMEM((chips, 2, per_dev, tile, cut), BF),
            pltpu.VMEM((group, gpart, width), F32),
            pltpu.VMEM((group, gpart, width), BF),
            pltpu.VMEM((group, gpart, width), BF),
            pltpu.VMEM((owners, prow, width), BF),
            pltpu.VMEM((chips, prow, width), BF),
            pltpu.VMEM((owners, prow, width), BF),
            pltpu.VMEM((group, owners, prow, width), BF),
            pltpu.VMEM((owners, prow, width), F32),
            dma(2, half, 2, per_dev), dma(2, half, 2, per_dev), dma(chips, 2), dma(chips, 2),
            dma(2, n_col), dma(2, n_col), dma(2, n_col), dma(2, n_col),
            dma(2, half, 2, per_dev), dma(2, half, 2, per_dev), dma(chips, 2), dma(chips, 2),
            dma(group), dma(group), dma(chips), dma(chips),
            dma(chips), dma(chips), dma(group), dma(group),
        ],
        compiler_params=pltpu.CompilerParams(
            collective_id=0, has_side_effects=True, vmem_limit_bytes=58 * 1024 * 1024
        ),
        name="graph_layer",
    )(
        features.reshape(per_dev, tile, width),
        weight,
        tile_values[0, 0],
        tile_rows[0, 0],
        tile_cols[0, 0],
        tile_count[0],
        cotangent,
    )
    return pl.pallas_call(
        write,
        out_shape=(
            jax.ShapeDtypeStruct((rows_dev, width), BF),
            jax.ShapeDtypeStruct((rows_dev, width), BF),
            jax.ShapeDtypeStruct((width, width), F32),
        ),
        in_specs=[vmem, vmem, vmem],
        out_specs=(vmem, vmem, vmem),
        name="write",
    )(act, gf, gw.reshape(width, width))


def solution(mesh):
    in_specs = (
        P(("row", "col"), None),
        P(),
        P("row", "col", None, None, None),
        P("row", "col", None),
        P("row", "col", None),
        P("row", "col"),
        P(("row", "col"), None),
    )
    out_specs = (P(("row", "col"), None), P(("row", "col"), None), P())
    return jax.shard_map(
        per_device, mesh=mesh, in_specs=in_specs, out_specs=out_specs, check_vma=False
    )
```
